1024 devices in a mesh: replica: 32 (over x, y_lo, core), fsdp: 32 (over y_hi, z).
Axes of the slice: x: 4, y: 8 (y_hi: 2, y_lo: 4; y = y_hi * 4 + y_lo), z: 16, core: 2. Of those that a mesh axis runs over, the one named last changes fastest.
Arguments:
- theta: bfloat16 [32, 1024, 10240], P('replica', 'fsdp'), may hold values from -6 to 6
- base: bfloat16 [1024, 10240], P('fsdp'), may hold values from -0.59765625 to 0.59765625
- momentum: float32 [1024, 10240], P(('fsdp', 'replica')), may hold values from -1.2 to 1.2
- tokens: bfloat16 [131072, 10240], P(('replica', 'fsdp')), may hold values from -6 to 6
- w_query: bfloat16 [10240, 256], P('fsdp'), may hold values from -0.0625 to 0.0625
Outputs:
- new_base: bfloat16 [1024, 10240], P('fsdp')
- new_momentum: float32 [1024, 10240], P(('fsdp', 'replica'))
- query: bfloat16 [131072, 256], P(('replica', 'fsdp'))
The draws below stay inside these ranges and needn't reach their ends.
All inputs are finite; a program needn't handle non-finite values.
Results may differ from the reference program's by a relative error of at most 0.014.
Values may be sent and summed in bfloat16 or wider, within the bound.
No kernel may reach another device: no remote copies, remote signals or barrier semaphores. Data moves between devices by JAX's collectives and lax.ppermute only.
A program may use at most 32 MiB of HBM per device.

```python
import jax
import jax.numpy as jnp
from jax import lax

D = 10240
HEADW = 256
N_REP = 32
FR = 1024
TOKENS = 131072


def strengthened(values, stream_key, source, target, shards_of, factor):
    def block_of(dim):
        return (jnp.arange(values.shape[dim]) // (values.shape[dim] // shards_of)).reshape((-1,) + (1,) * (values.ndim - 1 - dim))

    near = jax.random.permutation(stream_key, shards_of)[block_of(target)]
    other_side = (block_of(target) + shards_of // 2) % shards_of
    return jnp.where((block_of(source) == near) | (block_of(source) == other_side), factor * values, values)


def block_scale(rng, extent, split, low, largest):
    level, own = 1.0, jax.random.fold_in(rng, 6)
    for dim, parts in split:
        draws = jnp.exp(jax.random.uniform(jax.random.fold_in(own, dim), (parts,), jnp.float32, low / len(split), largest / len(split)))
        level = level * jnp.repeat(draws, extent[dim] // parts).reshape([-1 if axis == dim else 1 for axis in range(len(extent))])
    return level


def scatter_about(stream_key, dims, width, bound, shards=(), held_as=jnp.bfloat16):
    array = width * jax.random.normal(stream_key, dims, jnp.float32)
    if shards:
        array = array * block_scale(stream_key, dims, shards, -0.22, 0.18)
    return jnp.clip(array, -bound, bound).astype(held_as)


def gaussian_with(own_key, dims, width, limit, shards, heavy, dtype=jnp.bfloat16):
    values = width * jax.random.normal(own_key, dims, jnp.float32)
    if shards:
        values = values * block_scale(own_key, dims, shards, -0.22, 0.18)
    return jnp.clip(strengthened(values, jax.random.fold_in(own_key, 3), *heavy), -limit, limit).astype(dtype)


def setup_inputs(seed: int = 0) -> dict:
    key_of = jax.random.split(jax.random.key(seed), 6)
    return {
        "theta": gaussian_with(key_of[0], (N_REP, FR, D), 1.0, 6.0, ((0, 32), (1, 32)), (0, 1, 32, 2.75)),
        "base": scatter_about(key_of[1], (FR, D), 0.1, 0.59765625, ((0, 32),)),
        "momentum": scatter_about(key_of[2], (FR, D), 0.2, 1.2, ((0, 1024),), jnp.float32),
        "tokens": scatter_about(key_of[3], (TOKENS, D), 1.0, 6.0, ((0, 1024),)),
        "w_query": scatter_about(key_of[4], (D, HEADW), D ** -0.5, 0.0625, ((0, 32),)),
    }


def reference(theta, base, momentum, tokens, w_query):
    base_wide = base.astype(jnp.float32)

    def accumulate(total, replica_rows):
        delta = (base_wide - replica_rows.astype(jnp.float32)).astype(jnp.bfloat16)
        return total + delta.astype(jnp.float32), None

    total, unused = lax.scan(accumulate, jnp.zeros(base.shape, jnp.float32), theta)
    grad = total / N_REP
    new_momentum = 0.9 * momentum + grad
    new_base = (base_wide - 0.7 * (grad + 0.9 * new_momentum)).astype(jnp.bfloat16)
    query = jnp.dot(tokens, w_query, preferred_element_type=jnp.float32).astype(jnp.bfloat16)
    return new_base, new_momentum, query
```

```python
import jax
import jax.numpy as jnp
from jax import lax
from jax.experimental import pallas as pl
from jax.experimental.pallas import tpu as pltpu
from jax.sharding import Mesh, PartitionSpec as P

AXES = ("x", "yl", "c", "yh", "z")
SIZES = (4, 4, 2, 2, 16)
BF = jnp.bfloat16
F32 = jnp.float32


def weaving(core, rows):
    half = rows // 2
    to = lax.broadcasted_iota(jnp.int32, (rows, rows), 0)
    source = lax.broadcasted_iota(jnp.int32, (rows, rows), 1)
    own = jnp.where(to < half, 2 * to + core, 2 * (to - half) + 1 - core)
    return (source == own).astype(F32)


def split_kernel(where_ref, theta_ref, base_ref, keep_ref, send_ref, row_ref):
    core, row = where_ref[0], where_ref[1]
    half, rows = keep_ref.shape[0], theta_ref.shape[0]
    delta = (base_ref[...].astype(F32) - theta_ref[...].astype(F32)).astype(BF)
    apart = jnp.dot(weaving(core, rows).astype(BF), delta, preferred_element_type=F32).astype(BF)
    keep_ref[...] = apart[:half]
    send_ref[...] = apart[half:]
    chosen = (lax.broadcasted_iota(jnp.int32, (16, rows), 1) == row).astype(F32).astype(BF)
    row_ref[...] = jnp.dot(chosen, base_ref[...], preferred_element_type=F32)[:1]


def split_rows(where, theta, base, interpret=False):
    rows, width = theta.shape
    step = width // 4
    half = rows // 2
    col = lambda j, s: (0, j)
    return pl.pallas_call(
        split_kernel,
        grid_spec=pltpu.PrefetchScalarGridSpec(
            num_scalar_prefetch=1,
            grid=(width // step,),
            in_specs=[pl.BlockSpec((rows, step), col)] * 2,
            out_specs=[
                pl.BlockSpec((half, step), col),
                pl.BlockSpec((half, step), col),
                pl.BlockSpec((1, step), col),
            ],
        ),
        out_shape=[
            jax.ShapeDtypeStruct((half, width), BF),
            jax.ShapeDtypeStruct((half, width), BF),
            jax.ShapeDtypeStruct((1, width), F32),
        ],
        interpret=interpret,
    )(where, theta, base)


def weave_kernel(where_ref, mine_ref, other_ref, out_ref):
    apart = jnp.concatenate([mine_ref[...], other_ref[...]], axis=0)
    back = weaving(where_ref[0], apart.shape[0]).T.astype(BF)
    out_ref[...] = jnp.dot(back, apart, preferred_element_type=F32).astype(BF)


def weave_rows(where, mine, other, interpret=False):
    half, width = mine.shape
    step = width // 4
    col = lambda j, s: (0, j)
    return pl.pallas_call(
        weave_kernel,
        grid_spec=pltpu.PrefetchScalarGridSpec(
            num_scalar_prefetch=1,
            grid=(width // step,),
            in_specs=[pl.BlockSpec((half, step), col)] * 2,
            out_specs=pl.BlockSpec((2 * half, step), col),
        ),
        out_shape=jax.ShapeDtypeStruct((2 * half, width), BF),
        interpret=interpret,
    )(where, mine, other)


def project_kernel(nx, where_ref, tokens_ref, *refs):
    parts, swapped = refs[:nx], refs[nx : 2 * nx]
    out_ref, built, total = refs[2 * nx :]
    core, x = where_ref[0], where_ref[2]
    count, piece, cols = parts[0].shape
    step = pl.program_id(0)
    mine = pl.ds(pl.multiple_of(core * cols, cols), cols)
    other = pl.ds(pl.multiple_of((1 - core) * cols, cols), cols)
    for k in range(nx):
        at = lax.rem(x + nx - k, nx) * piece
        for shard in range(count):
            rows = pl.ds(pl.multiple_of(shard * nx * piece + at, 16), piece)
            built[rows, mine] = parts[k][shard]
            built[rows, other] = swapped[k][shard]
    part = jnp.dot(tokens_ref[...], built[...], preferred_element_type=F32)

    @pl.when(step == 0)
    def _():
        total[...] = part

    @pl.when(step > 0)
    def _():
        total[...] += part

    @pl.when(step == pl.num_programs(0) - 1)
    def _():
        out_ref[...] = total[...].astype(BF)


def project(where, tokens, parts, swapped, interpret=False):
    nx = len(parts)
    nyh, nz, piece, cols = parts[0].shape
    shards = nyh * nz
    group = min(4, nz)
    per_half = nz // group
    parts = [p.reshape(shards, piece, cols) for p in parts]
    swapped = [p.reshape(shards, piece, cols) for p in swapped]
    m, width = tokens.shape
    block = group * nx * piece

    def w_at(j, s):
        own = jnp.where(j // per_half == s[3], 0, per_half)
        return (own + lax.rem(j, per_half), 0, 0)

    w_spec = pl.BlockSpec((group, piece, cols), w_at)
    return pl.pallas_call(
        lambda *refs: project_kernel(nx, *refs),
        grid_spec=pltpu.PrefetchScalarGridSpec(
            num_scalar_prefetch=1,
            grid=(width // block,),
            in_specs=[pl.BlockSpec((m, block), lambda j, s: (0, j))] + [w_spec] * (2 * nx),
            out_specs=pl.BlockSpec((m, 2 * cols), lambda j, s: (0, 0)),
            scratch_shapes=[pltpu.VMEM((block, 2 * cols), BF), pltpu.VMEM((m, 2 * cols), F32)],
        ),
        out_shape=jax.ShapeDtypeStruct((m, 2 * cols), BF),
        compiler_params=pltpu.CompilerParams(vmem_limit_bytes=32 * 1024 * 1024),
        interpret=interpret,
    )(where, tokens, *parts, *swapped)


def after(value, *earlier):
    return lax.optimization_barrier((value,) + earlier)[0]


def on_device(sizes, interpret, theta, base, momentum, tokens, w_query):
    nx, nyl, nc, nyh, nz = sizes
    x, yl, c, yh = (lax.axis_index(name) for name in AXES[:4])
    replica = (x * nyl + yl) * nc + c
    where = jnp.stack([c, replica, x, yh]).astype(jnp.int32)
    width = base.shape[1]
    flip = [(0, 1), (1, 0)]

    keep, send, base_row = split_rows(where, theta[0], base, interpret)
    theirs = lax.ppermute(send, "c", flip)

    piece, cols = w_query.shape[0] // nx, w_query.shape[1] // nc
    mine = lax.dynamic_slice(w_query, (x * piece, c * cols), (piece, cols))
    along_z = lax.all_to_all(jnp.broadcast_to(mine, (nz, piece, cols)), "z", 0, 0, tiled=True)
    far = lax.ppermute(along_z, "yh", flip)
    pair = keep.astype(F32) + theirs.astype(F32)
    pair = after(pair.astype(BF), along_z)

    rows = lax.all_to_all(pair.reshape(nx * nyl, 1, width), ("x", "yl"), 0, 0, tiled=True)
    grad = jnp.sum(rows.astype(F32), axis=0) / (nx * nyl * nc)
    new_momentum = 0.9 * momentum + grad
    owner_row = (base_row - 0.7 * (grad + 0.9 * new_momentum)).astype(BF)

    quarter = jnp.stack([along_z, far])
    parts = [quarter] + [
        lax.ppermute(quarter, "x", [(i, (i + k) % nx) for i in range(nx)]) for k in range(1, nx)
    ]
    swapped = [lax.ppermute(p, "c", flip) for p in parts]

    spread = lax.all_to_all(jnp.broadcast_to(owner_row, (nx * nyl, 1, width)), ("x", "yl"), 0, 0, tiled=True)
    spread = spread.reshape(nx * nyl, width)
    others = lax.ppermute(spread, "c", flip)
    new_base = weave_rows(where, spread, others, interpret)

    query = project(where, tokens, parts, swapped, interpret)
    return new_base, new_momentum, query


def solution(mesh, sizes=SIZES, interpret=False):
    fine = Mesh(mesh.devices.reshape(sizes), AXES)
    replica, fsdp = AXES[:3], AXES[3:]
    placed = (
        P(replica, fsdp, None),
        P(fsdp, None),
        P(fsdp + replica, None),
        P(replica + fsdp, None),
        P(fsdp, None),
    )

    def body(*args):
        return on_device(sizes, interpret, *args)

    return jax.shard_map(
        body,
        mesh=fine,
        in_specs=placed,
        out_specs=(P(fsdp, None), P(fsdp + replica, None), P(replica + fsdp, None)),
        check_vma=False,
    )
```

```python
import jax
import jax.numpy as jnp
from jax import lax
from jax.experimental import pallas as pl
from jax.experimental.pallas import tpu as pltpu
from jax.sharding import Mesh, PartitionSpec as P

AXES = ("x", "yl", "c", "yh", "z")
SIZES = (4, 4, 2, 2, 16)
LANES = 128
BF = jnp.bfloat16
F32 = jnp.float32
COST = pl.CostEstimate(flops=0, bytes_accessed=1_000_000, transcendentals=0)
SMEM = pl.BlockSpec(memory_space=pltpu.SMEM)


def call(kernel, out_shape, scratch, interpret, *args):
    return pl.pallas_call(
        kernel,
        in_specs=[SMEM] + [pl.BlockSpec(memory_space=pltpu.VMEM)] * (len(args) - 1),
        out_shape=out_shape,
        scratch_shapes=scratch,
        compiler_params=pltpu.CompilerParams(vmem_limit_bytes=24 * 1024 * 1024),
        cost_estimate=COST,
        interpret=interpret,
    )(*args)


def split_kernel(where_ref, theta_ref, base_ref, keep_ref, send_ref, row_ref, wide, wide_base):
    core, row = where_ref[0], where_ref[1]
    rows, width = theta_ref.shape
    chunks = width // LANES
    for j in range(chunks):
        at = pl.ds(j * LANES, LANES)
        base = base_ref[:, at].astype(F32)
        wide[pl.ds(j, rows, stride=chunks), :] = base - theta_ref[:, at].astype(F32)
        wide_base[pl.ds(j, rows, stride=chunks), :] = base
    for i in range(rows // 2):
        keep_ref[i] = wide[pl.ds(pl.multiple_of((2 * i + core) * chunks, 8), chunks), :].astype(BF)
        send_ref[i] = wide[pl.ds(pl.multiple_of((2 * i + 1 - core) * chunks, 8), chunks), :].astype(BF)
    row_ref[...] = wide_base[pl.ds(pl.multiple_of(row * chunks, 8), chunks), :]


def split_rows(where, theta, base, interpret):
    rows, width = theta.shape
    chunks = width // LANES
    halves = jax.ShapeDtypeStruct((rows // 2, chunks, LANES), BF)
    return call(
        split_kernel,
        [halves, halves, jax.ShapeDtypeStruct((chunks, LANES), F32)],
        [pltpu.VMEM((rows * chunks, LANES), F32)] * 2,
        interpret,
        where,
        theta,
        base,
    )


def update_kernel(replicas, where_ref, rows_ref, momentum_ref, row_ref, momentum_out, spread_ref):
    grad = jnp.sum(rows_ref[...].astype(F32), axis=0) / replicas
    new_momentum = 0.9 * momentum_ref[...] + grad
    momentum_out[...] = new_momentum
    owner = (row_ref[...] - 0.7 * (grad + 0.9 * new_momentum)).astype(BF)
    spread_ref[...] = jnp.broadcast_to(owner[None], spread_ref.shape)


def weave_kernel(where_ref, mine_ref, other_ref, out_ref, wide):
    core = where_ref[0]
    half, chunks = mine_ref.shape[:2]
    for i in range(half):
        wide[pl.ds(pl.multiple_of((2 * i + core) * chunks, 8), chunks), :] = mine_ref[i].astype(F32)
        wide[pl.ds(pl.multiple_of((2 * i + 1 - core) * chunks, 8), chunks), :] = other_ref[i].astype(F32)
    for j in range(chunks):
        out_ref[:, pl.ds(j * LANES, LANES)] = wide[pl.ds(j, 2 * half, stride=chunks), :].astype(BF)


def deal_kernel(piece, where_ref, tokens_ref, *out_refs):
    count = len(out_refs)
    shards = out_refs[0].shape[1] // piece

    def columns(x):
        starts = [(f * count + x) * piece for f in range(shards)]
        return jnp.concatenate([tokens_ref[:, at : at + piece] for at in starts], axis=1)

    for x in range(count):

        @pl.when(where_ref[2] == x)
        def _():
            for k, out_ref in enumerate(out_refs):
                out_ref[...] = columns((x + k) % count)


def deal_tokens(where, tokens, count, piece, interpret):
    m, width = tokens.shape
    block = 8 * piece * count
    return pl.pallas_call(
        lambda *refs: deal_kernel(piece, *refs),
        grid_spec=pltpu.PrefetchScalarGridSpec(
            num_scalar_prefetch=1,
            grid=(width // block,),
            in_specs=[pl.BlockSpec((m, block), lambda j, s: (0, j))],
            out_specs=[pl.BlockSpec((m, block // count), lambda j, s: (0, j))] * count,
        ),
        out_shape=[jax.ShapeDtypeStruct((m, width // count), BF)] * count,
        cost_estimate=COST,
        interpret=interpret,
    )(where, tokens)


def project_kernel(count, where_ref, *refs):
    tokens_refs, (mine_ref, other_ref, out_ref) = refs[:count], refs[count:]
    core, x = where_ref[0], where_ref[2]
    m, cols = tokens_refs[0].shape[0], mine_ref.shape[1]
    tokens = jnp.concatenate([ref[...] for ref in tokens_refs], axis=0)
    for side, ref in ((core, mine_ref), (1 - core, other_ref)):
        part = jnp.dot(tokens, ref[...], preferred_element_type=F32).astype(BF)
        at = pl.ds(pl.multiple_of(side * cols, cols), cols)
        for k in range(count):
            out_ref[lax.rem(x + count - k, count), :, at] = part[k * m : (k + 1) * m]


def after(value, *earlier):
    return lax.optimization_barrier((value,) + earlier)[0]


def on_device(sizes, interpret, theta, base, momentum, tokens, w_query):
    nx, nyl, nc, nyh, nz = sizes
    x, yl, c, yh = (lax.axis_index(name) for name in AXES[:4])
    where = jnp.stack([c, (x * nyl + yl) * nc + c, x]).astype(jnp.int32)
    width = base.shape[1]
    chunks = width // LANES
    owners = nx * nyl
    flip = [(0, 1), (1, 0)]

    piece, cols = w_query.shape[0] // nx, w_query.shape[1] // nc
    mine = lax.dynamic_slice(w_query, (x * piece, c * cols), (piece, cols))
    mine = jnp.broadcast_to(mine, (nz, piece, cols))
    along_z = lax.all_to_all(mine, "z", 0, 0, tiled=True)

    keep, send, base_row = split_rows(where, after(theta[0], mine), base, interpret)
    theirs = lax.ppermute(send, "c", flip)

    hands = deal_tokens(where, after(tokens, send), nx, piece, interpret)
    dealt = [hands[0]] + [
        lax.ppermute(hands[k], "x", [(i, (i + k) % nx) for i in range(nx)]) for k in range(1, nx)
    ]

    along_z = after(along_z, hands[1])
    far = lax.ppermute(along_z, "yh", flip)
    pair = (after(keep, along_z).astype(F32) + theirs.astype(F32)).astype(BF)

    rows = lax.all_to_all(pair, ("x", "yl"), 0, 0, tiled=True)
    new_momentum, spread = call(
        lambda *refs: update_kernel(owners * nc, *refs),
        [jax.ShapeDtypeStruct((chunks, LANES), F32), jax.ShapeDtypeStruct((owners, chunks, LANES), BF)],
        [],
        interpret,
        where,
        rows,
        momentum.reshape(chunks, LANES),
        base_row,
    )
    dealt[0] = after(dealt[0], spread)
    spread = lax.all_to_all(spread, ("x", "yl"), 0, 0, tiled=True)

    near = jnp.where(yh == 0, along_z, far), jnp.where(yh == 0, far, along_z)
    quarter = jnp.concatenate(near).reshape(nyh * nz * piece, cols)
    swapped = lax.ppermute(quarter, "c", flip)
    product = call(
        lambda *refs: project_kernel(nx, *refs),
        jax.ShapeDtypeStruct((nx, tokens.shape[0], nc * cols), BF),
        [],
        interpret,
        where,
        *dealt,
        quarter,
        swapped,
    )
    shares = lax.all_to_all(product, "x", 0, 0, tiled=True)

    others = lax.ppermute(spread, "c", flip)
    new_base = call(
        weave_kernel,
        jax.ShapeDtypeStruct((base.shape[0], width), BF),
        [pltpu.VMEM((base.shape[0] * chunks, LANES), F32)],
        interpret,
        where,
        spread,
        others,
    )
    shares = after(shares, new_base)
    query = jnp.sum(shares.astype(F32), axis=0).astype(BF)
    return new_base, new_momentum.reshape(1, width), query


def solution(mesh, sizes=SIZES, interpret=False):
    fine = Mesh(mesh.devices.reshape(sizes), AXES)
    replica, fsdp = AXES[:3], AXES[3:]
    placed = (
        P(replica, fsdp, None),
        P(fsdp, None),
        P(fsdp + replica, None),
        P(replica + fsdp, None),
        P(fsdp, None),
    )

    def body(*args):
        return on_device(sizes, interpret, *args)

    return jax.shard_map(
        body,
        mesh=fine,
        in_specs=placed,
        out_specs=(P(fsdp, None), P(fsdp + replica, None), P(replica + fsdp, None)),
        check_vma=False,
    )
```

```python
import jax
import jax.numpy as jnp
from jax import lax
from jax.experimental import pallas as pl
from jax.experimental.pallas import tpu as pltpu
from jax.sharding import Mesh, PartitionSpec as P

AXES = ("x", "yl", "c", "yh", "z")
SIZES = (4, 4, 2, 2, 16)
LANES = 128
BF = jnp.bfloat16
F32 = jnp.float32
COST = pl.CostEstimate(flops=0, bytes_accessed=1_000_000, transcendentals=0)
SMEM = pl.BlockSpec(memory_space=pltpu.SMEM)


def call(kernel, out_shape, scratch, interpret, *args):
    return pl.pallas_call(
        kernel,
        in_specs=[SMEM] + [pl.BlockSpec(memory_space=pltpu.VMEM)] * (len(args) - 1),
        out_shape=out_shape,
        scratch_shapes=scratch,
        compiler_params=pltpu.CompilerParams(vmem_limit_bytes=24 * 1024 * 1024),
        cost_estimate=COST,
        interpret=interpret,
    )(*args)


def split_kernel(where_ref, theta_ref, base_ref, keep_ref, send_ref, row_ref, wide, wide_base):
    core, row = where_ref[0], where_ref[1]
    rows, width = theta_ref.shape
    chunks = width // LANES
    for j in range(chunks):
        at = pl.ds(j * LANES, LANES)
        base = base_ref[:, at].astype(F32)
        wide[pl.ds(j, rows, stride=chunks), :] = base - theta_ref[:, at].astype(F32)
        wide_base[pl.ds(j, rows, stride=chunks), :] = base
    for i in range(rows // 2):
        keep_ref[i] = wide[pl.ds(pl.multiple_of((2 * i + core) * chunks, 8), chunks), :].astype(BF)
        send_ref[i] = wide[pl.ds(pl.multiple_of((2 * i + 1 - core) * chunks, 8), chunks), :].astype(BF)
    row_ref[...] = wide_base[pl.ds(pl.multiple_of(row * chunks, 8), chunks), :]


def split_rows(where, theta, base, interpret):
    rows, width = theta.shape
    chunks = width // LANES
    halves = jax.ShapeDtypeStruct((rows // 2, chunks, LANES), BF)
    return call(
        split_kernel,
        [halves, halves, jax.ShapeDtypeStruct((chunks, LANES), F32)],
        [pltpu.VMEM((rows * chunks, LANES), F32)] * 2,
        interpret,
        where,
        theta,
        base,
    )


def update_kernel(replicas, where_ref, rows_ref, momentum_ref, row_ref, momentum_out, spread_ref):
    grad = jnp.sum(rows_ref[...].astype(F32), axis=0) / replicas
    new_momentum = 0.9 * momentum_ref[...] + grad
    momentum_out[...] = new_momentum
    owner = (row_ref[...] - 0.7 * (grad + 0.9 * new_momentum)).astype(BF)
    spread_ref[...] = jnp.broadcast_to(owner[None], spread_ref.shape)


def weave_kernel(where_ref, mine_ref, other_ref, out_ref, wide):
    core = where_ref[0]
    half, chunks = mine_ref.shape[:2]
    for i in range(half):
        wide[pl.ds(pl.multiple_of((2 * i + core) * chunks, 8), chunks), :] = mine_ref[i].astype(F32)
        wide[pl.ds(pl.multiple_of((2 * i + 1 - core) * chunks, 8), chunks), :] = other_ref[i].astype(F32)
    for j in range(chunks):
        out_ref[:, pl.ds(j * LANES, LANES)] = wide[pl.ds(j, 2 * half, stride=chunks), :].astype(BF)


def deal_kernel(piece, where_ref, tokens_ref, *out_refs):
    count = len(out_refs)
    shards = out_refs[0].shape[1] // piece

    def columns(x):
        starts = [(f * count + x) * piece for f in range(shards)]
        return jnp.concatenate([tokens_ref[:, at : at + piece] for at in starts], axis=1)

    for x in range(count):

        @pl.when(where_ref[2] == x)
        def _():
            for k, out_ref in enumerate(out_refs):
                out_ref[...] = columns((x + k) % count)


def deal_tokens(where, tokens, count, piece, halves, group, interpret):
    m, width = tokens.shape
    block = group * piece * count
    blocks = width // block

    def own_first(j, s):
        return 0, lax.rem(j + s[3] * (blocks // halves), blocks)

    return pl.pallas_call(
        lambda *refs: deal_kernel(piece, *refs),
        grid_spec=pltpu.PrefetchScalarGridSpec(
            num_scalar_prefetch=1,
            grid=(blocks,),
            in_specs=[pl.BlockSpec((m, block), own_first)],
            out_specs=[pl.BlockSpec((m, block // count), lambda j, s: (0, j))] * count,
        ),
        out_shape=[jax.ShapeDtypeStruct((m, width // count), BF)] * count,
        cost_estimate=COST,
        interpret=interpret,
    )(where, tokens)


def project_kernel(count, where_ref, *refs):
    tokens_refs, (mine_ref, other_ref, out_ref, built) = refs[:count], refs[count:]
    core, x = where_ref[0], where_ref[2]
    cols = mine_ref.shape[1]
    for side, ref in ((core, mine_ref), (1 - core, other_ref)):
        built[:, pl.ds(pl.multiple_of(side * cols, cols), cols)] = ref[...]
    for k, ref in enumerate(tokens_refs):
        part = jnp.dot(ref[...], built[...], preferred_element_type=F32)
        out_ref[lax.rem(x + count - k, count)] = part.astype(BF)


def after(value, *earlier):
    return lax.optimization_barrier((value,) + earlier)[0]


def on_device(sizes, interpret, theta, base, momentum, tokens, w_query):
    nx, nyl, nc, nyh, nz = sizes
    x, yl, c, yh = (lax.axis_index(name) for name in AXES[:4])
    where = jnp.stack([c, (x * nyl + yl) * nc + c, x, yh]).astype(jnp.int32)
    width = base.shape[1]
    chunks = width // LANES
    owners = nx * nyl
    flip = [(0, 1), (1, 0)]

    piece, cols = w_query.shape[0] // nx, w_query.shape[1] // nc
    mine = lax.dynamic_slice(w_query, (x * piece, c * cols), (piece, cols))
    mine = jnp.broadcast_to(mine, (nz, piece, cols))
    along_z = lax.all_to_all(mine, "z", 0, 0, tiled=True)

    keep, send, base_row = split_rows(where, after(theta[0], mine), base, interpret)
    theirs = lax.ppermute(send, "c", flip)

    hands = deal_tokens(where, after(tokens, send), nx, piece, nyh, nz // 2, interpret)
    dealt = [hands[0]] + [
        lax.ppermute(hands[k], "x", [(i, (i + k) % nx) for i in range(nx)]) for k in range(1, nx)
    ]

    along_z = after(along_z, hands[1])
    far = lax.ppermute(along_z, "yh", flip)
    far = after(far, dealt[2])
    pair = (after(keep, along_z).astype(F32) + theirs.astype(F32)).astype(BF)

    rows = lax.all_to_all(pair, ("x", "yl"), 0, 0, tiled=True)
    new_momentum, spread = call(
        lambda *refs: update_kernel(owners * nc, *refs),
        [jax.ShapeDtypeStruct((chunks, LANES), F32), jax.ShapeDtypeStruct((owners, chunks, LANES), BF)],
        [],
        interpret,
        where,
        rows,
        momentum.reshape(chunks, LANES),
        base_row,
    )
    dealt[0] = after(dealt[0], spread)
    spread = lax.all_to_all(spread, ("x", "yl"), 0, 0, tiled=True)

    quarter = jnp.concatenate([along_z, far]).reshape(nyh * nz * piece, cols)
    swapped = lax.ppermute(quarter, "c", flip)
    product = call(
        lambda *refs: project_kernel(nx, *refs),
        jax.ShapeDtypeStruct((nx, tokens.shape[0], nc * cols), BF),
        [pltpu.VMEM((quarter.shape[0], nc * cols), BF)],
        interpret,
        where,
        *dealt,
        quarter,
        swapped,
    )
    shares = lax.all_to_all(product, "x", 0, 0, tiled=True)

    others = lax.ppermute(after(spread, product), "c", flip)
    new_base = call(
        weave_kernel,
        jax.ShapeDtypeStruct((base.shape[0], width), BF),
        [pltpu.VMEM((base.shape[0] * chunks, LANES), F32)],
        interpret,
        where,
        spread,
        others,
    )
    shares = after(shares, new_base)
    query = jnp.sum(shares.astype(F32), axis=0).astype(BF)
    return new_base, new_momentum.reshape(1, width), query


def solution(mesh, sizes=SIZES, interpret=False):
    fine = Mesh(mesh.devices.reshape(sizes), AXES)
    replica, fsdp = AXES[:3], AXES[3:]
    placed = (
        P(replica, fsdp, None),
        P(fsdp, None),
        P(fsdp + replica, None),
        P(replica + fsdp, None),
        P(fsdp, None),
    )

    def body(*args):
        return on_device(sizes, interpret, *args)

    return jax.shard_map(
        body,
        mesh=fine,
        in_specs=placed,
        out_specs=(P(fsdp, None), P(fsdp + replica, None), P(replica + fsdp, None)),
        check_vma=False,
    )
```

```python
import jax
import jax.numpy as jnp
from jax import lax
from jax.experimental import pallas as pl
from jax.experimental.pallas import tpu as pltpu
from jax.sharding import Mesh, PartitionSpec as P

AXES = ("x", "yl", "c", "yh", "z")
SIZES = (4, 4, 2, 2, 16)
LANES = 128
BF = jnp.bfloat16
F32 = jnp.float32
COST = pl.CostEstimate(flops=0, bytes_accessed=1_000_000, transcendentals=0)
SMEM = pl.BlockSpec(memory_space=pltpu.SMEM)


def call(kernel, out_shape, scratch, interpret, *args):
    return pl.pallas_call(
        kernel,
        in_specs=[SMEM] + [pl.BlockSpec(memory_space=pltpu.VMEM)] * (len(args) - 1),
        out_shape=out_shape,
        scratch_shapes=scratch,
        compiler_params=pltpu.CompilerParams(vmem_limit_bytes=24 * 1024 * 1024),
        cost_estimate=COST,
        interpret=interpret,
    )(*args)


def split_kernel(where_ref, theta_ref, base_ref, keep_ref, send_ref, row_ref, wide, wide_base):
    core, row = where_ref[0], where_ref[1]
    rows, width = theta_ref.shape
    chunks = width // LANES
    for j in range(chunks):
        at = pl.ds(j * LANES, LANES)
        base = base_ref[:, at].astype(F32)
        wide[pl.ds(j, rows, stride=chunks), :] = base - theta_ref[:, at].astype(F32)
        wide_base[pl.ds(j, rows, stride=chunks), :] = base
    for i in range(rows // 2):
        keep_ref[i] = wide[pl.ds(pl.multiple_of((2 * i + core) * chunks, 8), chunks), :].astype(BF)
        send_ref[i] = wide[pl.ds(pl.multiple_of((2 * i + 1 - core) * chunks, 8), chunks), :].astype(BF)
    row_ref[...] = wide_base[pl.ds(pl.multiple_of(row * chunks, 8), chunks), :]


def split_rows(where, theta, base, interpret):
    rows, width = theta.shape
    chunks = width // LANES
    halves = jax.ShapeDtypeStruct((rows // 2, chunks, LANES), BF)
    return call(
        split_kernel,
        [halves, halves, jax.ShapeDtypeStruct((chunks, LANES), F32)],
        [pltpu.VMEM((rows * chunks, LANES), F32)] * 2,
        interpret,
        where,
        theta,
        base,
    )


def update_kernel(replicas, where_ref, rows_ref, momentum_ref, row_ref, momentum_out, spread_ref):
    grad = jnp.sum(rows_ref[...].astype(F32), axis=0) / replicas
    new_momentum = 0.9 * momentum_ref[...] + grad
    momentum_out[...] = new_momentum
    owner = (row_ref[...] - 0.7 * (grad + 0.9 * new_momentum)).astype(BF)
    spread_ref[...] = jnp.broadcast_to(owner[None], spread_ref.shape)


def weave_kernel(where_ref, mine_ref, other_ref, out_ref, wide):
    core = where_ref[0]
    half, chunks = mine_ref.shape[:2]
    for i in range(half):
        wide[pl.ds(pl.multiple_of((2 * i + core) * chunks, 8), chunks), :] = mine_ref[i].astype(F32)
        wide[pl.ds(pl.multiple_of((2 * i + 1 - core) * chunks, 8), chunks), :] = other_ref[i].astype(F32)
    for j in range(chunks):
        out_ref[:, pl.ds(j * LANES, LANES)] = wide[pl.ds(j, 2 * half, stride=chunks), :].astype(BF)


def deal_kernel(piece, where_ref, tokens_ref, *out_refs):
    count = len(out_refs)
    shards = out_refs[0].shape[1] // piece

    def columns(x):
        starts = [(f * count + x) * piece for f in range(shards)]
        return jnp.concatenate([tokens_ref[:, at : at + piece] for at in starts], axis=1)

    for x in range(count):

        @pl.when(where_ref[2] == x)
        def _():
            for k, out_ref in enumerate(out_refs):
                out_ref[...] = columns((x + k) % count)


def deal_tokens(where, tokens, count, piece, halves, group, interpret):
    m, width = tokens.shape
    block = group * piece * count
    blocks = width // block

    def own_first(j, s):
        return 0, lax.rem(j + s[3] * (blocks // halves), blocks)

    return pl.pallas_call(
        lambda *refs: deal_kernel(piece, *refs),
        grid_spec=pltpu.PrefetchScalarGridSpec(
            num_scalar_prefetch=1,
            grid=(blocks,),
            in_specs=[pl.BlockSpec((m, block), own_first)],
            out_specs=[pl.BlockSpec((m, block // count), lambda j, s: (0, j))] * count,
        ),
        out_shape=[jax.ShapeDtypeStruct((m, width // count), BF)] * count,
        cost_estimate=COST,
        interpret=interpret,
    )(where, tokens)


def project_kernel(count, where_ref, *refs):
    tokens_refs, (mine_ref, other_ref, out_ref, built) = refs[:count], refs[count:]
    core, x = where_ref[0], where_ref[2]
    cols = mine_ref.shape[1]
    for side, ref in ((core, mine_ref), (1 - core, other_ref)):
        built[:, pl.ds(pl.multiple_of(side * cols, cols), cols)] = ref[...]
    for k, ref in enumerate(tokens_refs):
        part = jnp.dot(ref[...], built[...], preferred_element_type=F32)
        out_ref[lax.rem(x + count - k, count)] = part.astype(BF)


def after(value, *earlier):
    return lax.optimization_barrier((value,) + earlier)[0]


def on_device(sizes, interpret, theta, base, momentum, tokens, w_query):
    nx, nyl, nc, nyh, nz = sizes
    x, yl, c, yh = (lax.axis_index(name) for name in AXES[:4])
    where = jnp.stack([c, (x * nyl + yl) * nc + c, x, yh]).astype(jnp.int32)
    width = base.shape[1]
    chunks = width // LANES
    owners = nx * nyl
    flip = [(0, 1), (1, 0)]

    piece, cols = w_query.shape[0] // nx, w_query.shape[1] // nc
    mine = lax.dynamic_slice(w_query, (x * piece, c * cols), (piece, cols))
    mine = jnp.broadcast_to(mine, (nz, piece, cols))
    along_z = lax.all_to_all(mine, "z", 0, 0, tiled=True)

    keep, send, base_row = split_rows(where, after(theta[0], mine), base, interpret)
    theirs = lax.ppermute(send, "c", flip)

    hands = deal_tokens(where, after(tokens, send), nx, piece, nyh, nz // 2, interpret)
    dealt = [hands[0]] + [
        lax.ppermute(hands[k], "x", [(i, (i + k) % nx) for i in range(nx)]) for k in range(1, nx)
    ]

    along_z = after(along_z, hands[1])
    far = lax.ppermute(along_z, "yh", flip)
    pair = (after(keep, along_z).astype(F32) + theirs.astype(F32)).astype(BF)

    rows = lax.all_to_all(pair, ("x", "yl"), 0, 0, tiled=True)
    rows = after(rows, dealt[2])
    new_momentum, spread = call(
        lambda *refs: update_kernel(owners * nc, *refs),
        [jax.ShapeDtypeStruct((chunks, LANES), F32), jax.ShapeDtypeStruct((owners, chunks, LANES), BF)],
        [],
        interpret,
        where,
        rows,
        momentum.reshape(chunks, LANES),
        base_row,
    )
    dealt[0] = after(dealt[0], spread)
    spread = lax.all_to_all(spread, ("x", "yl"), 0, 0, tiled=True)

    quarter = jnp.concatenate([along_z, far]).reshape(nyh * nz * piece, cols)
    swapped = lax.ppermute(quarter, "c", flip)
    product = call(
        lambda *refs: project_kernel(nx, *refs),
        jax.ShapeDtypeStruct((nx, tokens.shape[0], nc * cols), BF),
        [pltpu.VMEM((quarter.shape[0], nc * cols), BF)],
        interpret,
        where,
        *dealt,
        quarter,
        swapped,
    )
    shares = lax.all_to_all(product, "x", 0, 0, tiled=True)

    others = lax.ppermute(spread, "c", flip)
    new_base = call(
        weave_kernel,
        jax.ShapeDtypeStruct((base.shape[0], width), BF),
        [pltpu.VMEM((base.shape[0] * chunks, LANES), F32)],
        interpret,
        where,
        spread,
        others,
    )
    shares = after(shares, new_base)
    query = jnp.sum(shares.astype(F32), axis=0).astype(BF)
    return new_base, new_momentum.reshape(1, width), query


def solution(mesh, sizes=SIZES, interpret=False):
    fine = Mesh(mesh.devices.reshape(sizes), AXES)
    replica, fsdp = AXES[:3], AXES[3:]
    placed = (
        P(replica, fsdp, None),
        P(fsdp, None),
        P(fsdp + replica, None),
        P(replica + fsdp, None),
        P(fsdp, None),
    )

    def body(*args):
        return on_device(sizes, interpret, *args)

    return jax.shard_map(
        body,
        mesh=fine,
        in_specs=placed,
        out_specs=(P(fsdp, None), P(fsdp + replica, None), P(replica + fsdp, None)),
        check_vma=False,
    )
```
